32 devices in a mesh: band: 8 (over z, y), head: 4 (over x, core).
Axes of the slice: x: 2, y: 2, z: 4, core: 2. Of those that a mesh axis runs over, the one named last changes fastest.
Arguments:
- encoded: bfloat16 [4, 16, 128, 384], P('head', None, 'band'), may hold values from -6 to 6
- key_mask: int32 [8, 32], replicated, may hold values from 0 to 1, as said below
- first_gain: float32 [384], replicated, may hold values from 0.25 to 1.75
- first_bias: float32 [384], replicated, may hold values from -1.5 to 1.5
- query_conv: bfloat16 [9, 384], replicated, may hold values from -2 to 2
- query_weight: bfloat16 [384, 384], replicated, may hold values from -0.3125 to 0.3125
- key_weight: bfloat16 [384, 384], replicated, may hold values from -1.25 to 1.25
- value_weight: bfloat16 [384, 384], replicated, may hold values from -0.875 to 0.875
- output_weight: bfloat16 [384, 384], replicated, may hold values from -5 to 5
- second_gain: float32 [384], replicated, may hold values from 0.25 to 1.75
- second_bias: float32 [384], replicated, may hold values from -1.5 to 1.5
- up_weight: bfloat16 [384, 1536], replicated, may hold values from -0.3125 to 0.3125
- hidden_conv: bfloat16 [9, 1536], replicated, may hold values from -2 to 2
- down_weight: bfloat16 [1536, 384], replicated, may hold values from -0.15625 to 0.15625
- cotangent: bfloat16 [4, 32, 256, 384], P('head', 'band'), may hold values from -6 to 6
Outputs:
- decoded: bfloat16 [4, 32, 256, 384], P('head', 'band')
- encoded_grad: bfloat16 [4, 16, 128, 384], P('head', None, 'band')
- first_gain_grad: float32 [384], replicated
- first_bias_grad: float32 [384], replicated
- query_conv_grad: float32 [9, 384], replicated
- query_weight_grad: float32 [384, 384], replicated
- key_weight_grad: float32 [384, 384], replicated
- value_weight_grad: float32 [384, 384], replicated
- output_weight_grad: float32 [384, 384], replicated
- second_gain_grad: float32 [384], replicated
- second_bias_grad: float32 [384], replicated
- up_weight_grad: float32 [384, 1536], replicated
- hidden_conv_grad: float32 [9, 1536], replicated
- down_weight_grad: float32 [1536, 384], replicated
The draws below stay inside these ranges and needn't reach their ends.
Inputs may be any that keep to these rules, and one draw needn't show every extreme that they name: Row r of key_mask is 1 in its first w_r columns and 0 after them, with 16 <= w_r < 32, each row with its own w_r.
All inputs are finite; a program needn't handle non-finite values.
Results may differ from the reference program's by a relative error of at most 0.035.
Values may be sent and summed in bfloat16 or wider, within the bound.
A program may use at most 256 MiB of HBM per device.

```python
from functools import partial
import jax
import jax.numpy as jnp
from jax import lax

D = 384
HEADS = 6
F = 1536
W16 = 128
POOLR = 4
POOLC = 8
HD = 64
TASKS = 4
H16 = 16
H8 = 32
W8 = 256
HP = 8
WP = 32
KEYS = 1024


def draw_key_mask(key, part):
    key = jax.random.fold_in(key, 7)
    row_widths = jax.random.randint(key, (HP, 1), WP // 2, WP)
    columns = lax.broadcasted_iota(jnp.int32, (HP, WP), 1)
    return (columns < row_widths).astype(jnp.int32)


def shard_levels(rng, shape, pieces, least, top_value):
    gain, own = 1.0, jax.random.fold_in(rng, 6)
    for axis_at, shards_of in pieces:
        heights = jnp.exp(jax.random.uniform(jax.random.fold_in(own, axis_at), (shards_of,), jnp.float32, least / len(pieces), top_value / len(pieces)))
        gain = gain * jnp.repeat(heights, shape[axis_at] // shards_of).reshape([-1 if axis == axis_at else 1 for axis in range(len(shape))])
    return gain


def centred(own_key, extent, scale, bound, split=(), held_as=jnp.bfloat16):
    drawn = jax.random.normal(own_key, extent, jnp.float32) * scale
    if len(split) > 0:
        drawn = shard_levels(own_key, extent, split, -0.22, 0.18) * drawn
    return jnp.clip(drawn, min=-bound, max=bound).astype(held_as)


def setup_inputs(seed: int = 0) -> dict:
    splits = jax.random.split(jax.random.key(seed), 16)
    return {
        "encoded": centred(splits[0], (TASKS, H16, W16, D), 1.0, 6.0, ((0, 4), (2, 8))),
        "key_mask": draw_key_mask(jax.random.fold_in(splits[15], 71), 0),
        "first_gain": jnp.clip(1.0 + 0.15 * jax.random.normal(splits[2], (D,), jnp.float32), 0.25, 1.75),
        "first_bias": centred(splits[3], (D,), 0.3, 1.5, (), jnp.float32),
        "query_conv": centred(splits[4], (9, D), 9 ** -0.5, 2.0),
        "query_weight": centred(splits[5], (D, D), D ** -0.5, 0.3125),
        "key_weight": centred(splits[6], (D, D), (D / 16) ** -0.5, 1.25),
        "value_weight": centred(splits[7], (D, D), (D / 8) ** -0.5, 0.875),
        "output_weight": centred(splits[8], (D, D), (max(1, 4 * D / KEYS)) ** -0.5, 5.0),
        "second_gain": jnp.clip(1.0 + 0.15 * jax.random.normal(splits[9], (D,), jnp.float32), 0.25, 1.75),
        "second_bias": centred(splits[10], (D,), 0.3, 1.5, (), jnp.float32),
        "up_weight": centred(splits[11], (D, F), D ** -0.5, 0.3125),
        "hidden_conv": centred(splits[12], (9, F), 9 ** -0.5, 2.0),
        "down_weight": centred(splits[13], (F, D), F ** -0.5, 0.15625),
        "cotangent": centred(splits[14], (TASKS, H8, W8, D), 1.0, 6.0, ((0, 4), (1, 8))),
    }


epsilon = 1e-06
block_rows = 2048

@jax.custom_vjp
def low(v):
    return lax.optimization_barrier(v.astype(jnp.bfloat16)).astype(jnp.float32)

@jax.custom_vjp
def low_back(v):
    return v

def low_keep(v):
    return (low(v), None)

def low_pass(kept, grad):
    return (grad,)

def back_keep(v):
    return (v, None)

def back_low(kept, grad):
    return (low(grad),)
low.defvjp(low_keep, low_pass)
low_back.defvjp(back_keep, back_low)

def dense(left, right):
    return jnp.dot(left, right, precision=lax.Precision.HIGHEST, preferred_element_type=jnp.float32)

def layer_norm(values, gain_vec, bias_vec):
    average = lax.optimization_barrier(jnp.mean(values, axis=-1, keepdims=True))
    centered = values - average
    variance = lax.optimization_barrier(jnp.mean(centered * centered, axis=-1, keepdims=True))
    return centered * lax.rsqrt(variance + epsilon) * gain_vec + bias_vec

def depthwise(field, kernel):
    height = field.shape[1]
    width = field.shape[2]
    padded = jnp.pad(field, ((0, 0), (1, 1), (1, 1), (0, 0)))
    summed = jnp.zeros(field.shape, jnp.float32)
    for offset in range(9):
        row_shift = offset // 3
        col_shift = offset % 3
        summed = summed + padded[:, row_shift:row_shift + height, col_shift:col_shift + width] * kernel[offset]
    return summed

def attention(queries, key_rows, value_rows, key_open):
    score_scale = HD ** (-0.5)
    key_heads = key_rows.reshape(KEYS, HEADS, HD)
    value_heads = value_rows.reshape(KEYS, HEADS, HD)
    query_blocks = queries.reshape(-1, block_rows, HEADS, HD)

    def one_block(query_part):
        scores = jnp.einsum('qhd,khd->hqk', query_part, key_heads, precision=lax.Precision.HIGHEST) * score_scale
        scores = low_back(scores)
        scores = jnp.where(key_open[None, None, :], scores, -1000000000.0)
        highest = lax.optimization_barrier(jnp.max(scores, axis=-1, keepdims=True))
        weights = jnp.exp(scores - highest)
        weights_low = low(weights / lax.optimization_barrier(jnp.sum(weights, axis=-1, keepdims=True)))
        mixed_heads = jnp.einsum('hqk,khd->qhd', weights_low, value_heads, precision=lax.Precision.HIGHEST)
        return mixed_heads.reshape(block_rows, D)
    return lax.map(jax.checkpoint(one_block), query_blocks).reshape(-1, D)

def forward(key_open, encoded, first_gain, first_bias, query_conv, query_weight, key_weight, value_weight, output_weight, second_gain, second_bias, up_weight, hidden_conv, down_weight):
    upsampled = jnp.repeat(jnp.repeat(encoded, 2, axis=1), 2, axis=2)
    normed = low(layer_norm(upsampled, first_gain, first_bias))
    conv_query = low(low_back(depthwise(normed, query_conv)))
    queries = low(low_back(dense(conv_query.reshape(-1, D), query_weight)))
    pooled = lax.optimization_barrier(jnp.mean(normed.reshape(TASKS, HP, POOLR, WP, POOLC, D), axis=(2, 4)))
    pooled = low(pooled.reshape(KEYS, D))
    key_rows = low(dense(pooled, key_weight))
    value_rows = low(dense(pooled, value_weight))
    attended = low(low_back(attention(queries, key_rows, value_rows, key_open)))
    branch = low_back(dense(attended, output_weight))
    middle = upsampled + branch.reshape(upsampled.shape)
    second = low(layer_norm(middle, second_gain, second_bias))
    hidden = low(low_back(dense(second.reshape(-1, D), up_weight)))
    spread = low_back(depthwise(hidden.reshape(TASKS, H8, W8, F), hidden_conv))
    activated = low(jax.nn.gelu(spread))
    output_branch = low_back(dense(activated.reshape(-1, F), down_weight))
    return middle + output_branch.reshape(middle.shape)

def reference(encoded, key_mask, first_gain, first_bias, query_conv, query_weight, key_weight, value_weight, output_weight, second_gain, second_bias, up_weight, hidden_conv, down_weight, cotangent):
    key_open = jnp.broadcast_to((key_mask > 0)[None], (TASKS, HP, WP)).reshape(KEYS)
    inputs = (encoded.astype(jnp.float32), first_gain.astype(jnp.float32), first_bias.astype(jnp.float32), query_conv.astype(jnp.float32), query_weight.astype(jnp.float32), key_weight.astype(jnp.float32), value_weight.astype(jnp.float32), output_weight.astype(jnp.float32), second_gain.astype(jnp.float32), second_bias.astype(jnp.float32), up_weight.astype(jnp.float32), hidden_conv.astype(jnp.float32), down_weight.astype(jnp.float32))
    result, pullback = jax.vjp(partial(forward, key_open), *inputs)
    grads = pullback(cotangent.astype(jnp.float32))
    return (result.astype(jnp.bfloat16), grads[0].astype(jnp.bfloat16), grads[1], grads[2], grads[3], grads[4], grads[5], grads[6], grads[7], grads[8], grads[9], grads[10], grads[11], grads[12])
```

```python
import functools
import math

import jax
import jax.numpy as jnp
from jax import lax
from jax.experimental import pallas as pl
from jax.experimental.pallas import tpu as pltpu
from jax.sharding import PartitionSpec as P

HEADS = 6
POOLR = 4
POOLC = 8
epsilon = 1e-06
f32 = jnp.float32
bf16 = jnp.bfloat16
VMEM = 60 << 20
MESH = pl.DeviceIdType.MESH


def dot(left, right, left_dim=1, right_dim=0):
    return lax.dot_general(
        left, right, (((left_dim,), (right_dim,)), ((), ())), preferred_element_type=f32
    )


def identity(size):
    rows = lax.broadcasted_iota(jnp.int32, (size, size), 0)
    cols = lax.broadcasted_iota(jnp.int32, (size, size), 1)
    return (rows == cols).astype(bf16)


def flipped(matrix):
    return matrix.T


def norm_parts(values):
    average = jnp.mean(values, axis=-1, keepdims=True)
    centered = values - average
    variance = jnp.mean(centered * centered, axis=-1, keepdims=True)
    inverse = lax.rsqrt(variance + epsilon)
    return centered * inverse, inverse


def norm_input_grad(upstream, unit_part, inverse, gain):
    scaled = upstream * gain
    average = jnp.mean(scaled, axis=-1, keepdims=True)
    projected = jnp.mean(scaled * unit_part, axis=-1, keepdims=True)
    return inverse * (scaled - average - unit_part * projected)


def from_left(block):
    rolled = pltpu.roll(block, 1, 0)
    rows = lax.broadcasted_iota(jnp.int32, block.shape, 0)
    return jnp.where(rows == 0, 0.0, rolled)


def from_right(block):
    count = block.shape[0]
    rolled = pltpu.roll(block, count - 1, 0)
    rows = lax.broadcasted_iota(jnp.int32, block.shape, 0)
    return jnp.where(rows == count - 1, 0.0, rolled)


def phase_order(width):
    half = width // 2
    rows = lax.broadcasted_iota(jnp.int32, (width, width), 0)
    cols = lax.broadcasted_iota(jnp.int32, (width, width), 1)
    wanted = jnp.where(rows < half, 2 * rows, 2 * (rows - half) + 1)
    return (cols == wanted).astype(bf16)


def split_three(values):
    high = values.astype(bf16)
    rest = values - high.astype(f32)
    middle = rest.astype(bf16)
    low = (rest - middle.astype(f32)).astype(bf16)
    return high, middle, low


def border_flags(dtype=f32):
    band = lax.axis_index("band")
    count = lax.axis_size("band")
    above = (band > 0).astype(dtype)
    below = (band < count - 1).astype(dtype)
    return above, below


def poly_weights(kernel):
    taps = [[kernel[3 * i + j : 3 * i + j + 1] for j in range(3)] for i in range(3)]
    row_sets = [{-1: [0], 0: [1, 2]}, {0: [0, 1], 1: [2]}]
    out = []
    for a in range(2):
        for b in range(2):
            entry = {}
            for di, rows in row_sets[a].items():
                for dj, cols in row_sets[b].items():
                    entry[(di, dj)] = functools.reduce(
                        lambda x, y: x + y, [taps[i][j] for i in rows for j in cols]
                    )
            out.append(entry)
    return out


def queries_kernel_part(enc_ref, gain, bias, conv_w, conv_ref):
    above, below = border_flags()
    rows = []
    for e in range(enc_ref.shape[0]):
        unit, _ = norm_parts(enc_ref[e].astype(f32))
        z = (unit * gain + bias).astype(bf16).astype(f32)
        if e == 0:
            z = z * above
        if e == enc_ref.shape[0] - 1:
            z = z * below
        rows.append((z, from_left(z), from_right(z)))
    weights = poly_weights(conv_w)
    half = rows[0][0].shape[0]
    at = 0
    for i in range(enc_ref.shape[0] - 2):
        for a in range(2):
            for b in range(2):
                total = None
                for (di, dj), w in weights[2 * a + b].items():
                    z = rows[1 + i + di][{0: 0, -1: 1, 1: 2}[dj]]
                    total = z * w if total is None else total + z * w
                conv_ref[at : at + half] = total.astype(bf16)
                at += half
    return rows


def key_blocks(pooled, key_t, aux):
    doubled = jnp.concatenate([key_t, key_t], axis=0)
    return jnp.concatenate([dot(pooled, doubled, 1, 1).astype(bf16), aux], axis=1)


def attend_kernel(
    enc_ref, pooled_ref, aux_ref, gain_ref, bias_ref, conv_ref, wq_ref, wk_ref, wv_ref, wo_ref,
    gain2_ref, bias2_ref,
    convq_ref, queries_ref, attended_ref, lse_ref, middle_ref, second_ref,
    wkt_ref, wvt_ref, qaug_ref, att_ref,
):
    keys = pooled_ref.shape[0]
    width = wq_ref.shape[0]
    tokens = convq_ref.shape[0]
    size = width // HEADS
    block = max(128, min(tokens, (1 << 20) // keys))
    queries_kernel_part(enc_ref, gain_ref[...], bias_ref[...], conv_ref[...].astype(f32), convq_ref)
    wkt_ref[...] = flipped(wk_ref[...])
    wvt_ref[...] = flipped(wv_ref[...])
    queries_t = dot(flipped(wq_ref[...]), convq_ref[...], 1, 1).astype(bf16)
    queries_ref[...] = queries_t
    factor = size ** (-0.5) * math.log2(math.e)
    ones_row = (lax.broadcasted_iota(jnp.int32, (size * 2, tokens), 0) == 0).astype(bf16)

    def head_step(h, carry):
        rows = pl.ds(pl.multiple_of(h * size, size), size)
        scaled = queries_ref[rows].astype(f32) * factor
        high = scaled.astype(bf16)
        low = (scaled - high.astype(f32)).astype(bf16)
        qaug_ref[...] = jnp.concatenate([high, low, ones_row], axis=0)
        key_aug = key_blocks(pooled_ref[...], wkt_ref[rows], aux_ref[...])
        value_t = dot(wvt_ref[rows], pooled_ref[...], 1, 1).astype(bf16)
        extra = (lax.broadcasted_iota(jnp.int32, (16, keys), 0) == 0).astype(bf16)
        value_aug = jnp.concatenate([value_t, extra], axis=0)
        for start in range(0, tokens, block):
            part = slice(start, start + block)
            scores = dot(key_aug, qaug_ref[:, part])
            top = jnp.max(scores, axis=0, keepdims=True)
            probs = jnp.exp2(scores - top).astype(bf16)
            mixed = dot(value_aug, probs)
            total = mixed[size : size + 1]
            att_ref[rows, part] = (mixed[:size] / total).astype(bf16)
            lse_ref[h, :, part] = jnp.broadcast_to(top + jnp.log2(total), (8, block))
        return carry

    lax.fori_loop(0, HEADS, head_step, 0)
    attended_ref[...] = att_ref[...]
    half = enc_ref.shape[1]
    for block_at in range(tokens // half):
        part = slice(block_at * half, (block_at + 1) * half)
        row = block_at // 4
        middle = enc_ref[1 + row].astype(f32) + dot(flipped(att_ref[:, part]), wo_ref[...])
        middle_ref[part] = middle
        unit, _ = norm_parts(middle)
        second_ref[part] = (unit * gain2_ref[...] + bias2_ref[...]).astype(bf16)


def attend(enc_ext, pooled_all, aux, gain, bias, conv_w, wq, wk, wv, wo, gain2, bias2):
    rows, half, width = enc_ext.shape
    tokens = (rows - 2) * 4 * half
    keys = pooled_all.shape[0]
    size = width // HEADS
    shapes = [
        jax.ShapeDtypeStruct((tokens, width), bf16),
        jax.ShapeDtypeStruct((width, tokens), bf16),
        jax.ShapeDtypeStruct((width, tokens), bf16),
        jax.ShapeDtypeStruct((HEADS, 8, tokens), f32),
        jax.ShapeDtypeStruct((tokens, width), f32),
        jax.ShapeDtypeStruct((tokens, width), bf16),
    ]
    return pl.pallas_call(
        attend_kernel,
        out_shape=shapes,
        scratch_shapes=[
            pltpu.VMEM((width, width), bf16),
            pltpu.VMEM((width, width), bf16),
            pltpu.VMEM((4 * size, tokens), bf16),
            pltpu.VMEM((width, tokens), bf16),
        ],
        compiler_params=pltpu.CompilerParams(vmem_limit_bytes=VMEM),
        name="attend_forward",
    )(enc_ext, pooled_all, aux, gain, bias, conv_w, wq, wk, wv, wo, gain2, bias2)


def gelu_both(x):
    scale = math.sqrt(2.0 / math.pi)
    square = x * x
    inner = x * (scale + (scale * 0.044715) * square)
    t = jnp.tanh(inner)
    half = 0.5 * (1.0 + t)
    slope = half + (0.5 * x) * (1.0 - t * t) * (scale + (3.0 * scale * 0.044715) * square)
    return x * half, slope


def forward_kernel(
    own_ref, low_ref, high_ref, middle_ref, cot_ref, up_ref, hconv_ref, down_ref,
    decoded_ref, cotp_ref, sgrad_ref, upg_ref, downg_ref, hcg_ref,
    ext_ref, extt_ref, cott_ref, dec_ref, hid_ref, spr_ref,
):
    step = pl.program_id(0)
    steps = pl.num_programs(0)
    rows = cot_ref.shape[1]
    width = cot_ref.shape[2]
    half = width // 2
    tokens = rows * width

    @pl.when(step == 0)
    def _():
        ext_ref[0:width] = low_ref[...]
        ext_ref[width : width + tokens] = own_ref[...]
        ext_ref[width + tokens :] = high_ref[...]
        order = phase_order(width)
        for r in range(rows):
            cotp_ref[r * width : (r + 1) * width] = dot(order, cot_ref[0, r]).astype(bf16)
        for r in range(rows + 2):
            part = slice(r * width, (r + 1) * width)
            extt_ref[:, part] = flipped(ext_ref[part])
        for r in range(rows):
            part = slice(r * width, (r + 1) * width)
            cott_ref[:, part] = flipped(cotp_ref[part])
        dec_ref[...] = middle_ref[...]
        sgrad_ref[...] = jnp.zeros_like(sgrad_ref)

    up = up_ref[...]
    down = down_ref[...]
    weights = hconv_ref[...].astype(f32)
    taps = [[weights[3 * i + j : 3 * i + j + 1] for j in range(3)] for i in range(3)]
    hid_ref[...] = dot(ext_ref[...], up).astype(bf16)

    def phases(ref, r):
        even = ref[r * width : r * width + half].astype(f32)
        odd = ref[r * width + half : (r + 1) * width].astype(f32)
        return even, odd, from_left(odd), from_right(even)

    hid = [phases(hid_ref, r) for r in range(rows + 2)]
    act_grad = dot(cotp_ref[...], down, 1, 1)
    hcg = [[0.0] * 3 for _ in range(3)]
    acts = []
    grads = []
    for r in range(rows):
        for b in range(2):
            spread = None
            for i in range(3):
                even, odd, odd_left, even_right = hid[r + i]
                three = (odd_left, even, odd) if b == 0 else (even, odd, even_right)
                for j in range(3):
                    term = three[j] * taps[i][j]
                    spread = term if spread is None else spread + term
            act, slope = gelu_both(spread)
            at = r * width + b * half
            sg = (act_grad[at : at + half] * slope).astype(bf16)
            acts.append(act.astype(bf16))
            grads.append(sg)
            sgf = sg.astype(f32)
            for i in range(3):
                even, odd, odd_left, even_right = hid[r + i]
                three = (odd_left, even, odd) if b == 0 else (even, odd, even_right)
                for j in range(3):
                    hcg[i][j] = hcg[i][j] + jnp.sum(sgf * three[j], axis=0, keepdims=True)
    act_all = jnp.concatenate(acts, axis=0)
    dec_ref[...] += dot(act_all, down)
    downg_ref[...] = dot(cott_ref[...], act_all).astype(bf16)
    hcg_ref[...] = jnp.concatenate([hcg[i][j] for i in range(3) for j in range(3)], axis=0)
    spr = []
    for r in range(rows):
        even = grads[2 * r].astype(f32)
        odd = grads[2 * r + 1].astype(f32)
        spr.append((even, odd, from_left(odd), from_right(even)))
    for r in range(-1, rows + 1):
        for b in range(2):
            total = None
            for i in range(3):
                source = r - i + 1
                if source < 0 or source >= rows:
                    continue
                even, odd, odd_left, even_right = spr[source]
                three = (odd, even, odd_left) if b == 0 else (even_right, odd, even)
                for j in range(3):
                    term = three[j] * taps[i][j]
                    total = term if total is None else total + term
            at = (r + 1) * width + b * half
            spr_ref[at : at + half] = total.astype(bf16)
    hid_grad = spr_ref[...]
    sgrad_ref[...] += dot(hid_grad, up, 1, 1)
    upg_ref[...] = dot(extt_ref[...], hid_grad).astype(bf16)

    @pl.when(step == steps - 1)
    def _():
        order = phase_order(width)
        for r in range(rows):
            part = slice(r * width, (r + 1) * width)
            decoded_ref[0, r] = dot(order, dec_ref[part].astype(bf16), 0, 0).astype(bf16)


def feed_forward(own, low, high, middle, cot, up, hconv, down):
    tokens, model = own.shape
    _, rows, width, _ = cot.shape
    hidden = up.shape[1]
    chunk = 256
    whole = lambda *shape: pl.BlockSpec(shape, lambda s: (0,) * len(shape))
    return pl.pallas_call(
        forward_kernel,
        grid=(hidden // chunk,),
        in_specs=[
            whole(tokens, model), whole(width, model), whole(width, model), whole(tokens, model),
            whole(1, rows, width, model),
            pl.BlockSpec((model, chunk), lambda s: (0, s)),
            pl.BlockSpec((9, chunk), lambda s: (0, s)),
            pl.BlockSpec((chunk, model), lambda s: (s, 0)),
        ],
        out_specs=[
            whole(1, rows, width, model), whole(tokens, model), whole(tokens + 2 * width, model),
            pl.BlockSpec((model, chunk), lambda s: (0, s)),
            pl.BlockSpec((model, chunk), lambda s: (0, s)),
            pl.BlockSpec((9, chunk), lambda s: (0, s)),
        ],
        out_shape=[
            jax.ShapeDtypeStruct((1, rows, width, model), bf16),
            jax.ShapeDtypeStruct((tokens, model), bf16),
            jax.ShapeDtypeStruct((tokens + 2 * width, model), f32),
            jax.ShapeDtypeStruct((model, hidden), bf16),
            jax.ShapeDtypeStruct((model, hidden), bf16),
            jax.ShapeDtypeStruct((9, hidden), f32),
        ],
        scratch_shapes=[
            pltpu.VMEM((tokens + 2 * width, model), bf16),
            pltpu.VMEM((model, tokens + 2 * width), bf16),
            pltpu.VMEM((model, tokens), bf16),
            pltpu.VMEM((tokens, model), f32),
            pltpu.VMEM((tokens + 2 * width, chunk), bf16),
            pltpu.VMEM((tokens + 2 * width, chunk), bf16),
        ],
        compiler_params=pltpu.CompilerParams(vmem_limit_bytes=VMEM),
        name="feed_forward",
    )(own, low, high, middle, cot, up, hconv, down)


def attend_back_kernel(
    enc_ref, pooled_ref, aux_ref, gain_ref, bias_ref, conv_ref, wq_ref, wk_ref, wv_ref, wo_ref,
    gain2_ref, convq_ref, queries_ref, attended_ref, lse_ref, middle_ref, cotp_ref, sgrad_ref,
    fromlow_ref, fromhigh_ref,
    enc_out, pooled_out, owg_ref, qwg_ref, kwg_ref, vwg_ref, vec_ref,
    wkt_ref, wvt_ref, qaug_ref, mgrad_ref, mlow_ref, agrad_ref, dq_ref, dk_ref, dv_ref, cg_ref,
):
    keys = pooled_ref.shape[0]
    tokens, width = convq_ref.shape
    size = width // HEADS
    half = enc_ref.shape[1]
    wide = 2 * half
    block = min(keys, 1024)
    gain2 = gain2_ref[...]
    gain2_sum = jnp.zeros((1, width), f32)
    bias2_sum = jnp.zeros((1, width), f32)
    rows = tokens // wide
    for r in range(rows):
        part = slice(r * wide, (r + 1) * wide)
        y = sgrad_ref[(r + 1) * wide : (r + 2) * wide]
        if r == 0:
            y = y + fromlow_ref[...].astype(f32)
        if r == rows - 1:
            y = y + fromhigh_ref[...].astype(f32)
        unit, inverse = norm_parts(middle_ref[part])
        gain2_sum += jnp.sum(y * unit, axis=0, keepdims=True)
        bias2_sum += jnp.sum(y, axis=0, keepdims=True)
        grad = cotp_ref[part].astype(f32) + norm_input_grad(y, unit, inverse, gain2)
        mgrad_ref[part] = grad
        mlow_ref[part] = grad.astype(bf16)
    owg_ref[...] = dot(attended_ref[...], mlow_ref[...]).astype(bf16)
    agrad_ref[...] = dot(wo_ref[...], mlow_ref[...], 1, 1).astype(bf16)
    wkt_ref[...] = flipped(wk_ref[...])
    wvt_ref[...] = flipped(wv_ref[...])
    scale = size ** (-0.5)
    factor = scale * math.log2(math.e)
    row_at = lax.broadcasted_iota(jnp.int32, (2 * size, tokens), 0)
    small_at = lax.broadcasted_iota(jnp.int32, (size, tokens), 0)
    lane = lax.broadcasted_iota(jnp.int32, (block, size), 1)
    three_ones = (lane < 3).astype(bf16)

    def place(at, first, values):
        total = jnp.zeros(at.shape, f32)
        for n, value in enumerate(values):
            total = jnp.where(at == first + n, value.astype(f32), total)
        return total

    def head_step(h, carry):
        part_rows = pl.ds(pl.multiple_of(h * size, size), size)
        head_queries = queries_ref[part_rows]
        scaled = head_queries.astype(f32) * factor
        high = scaled.astype(bf16)
        low = (scaled - high.astype(f32)).astype(bf16)
        lse = lse_ref[h, 0:1, :]
        extra = place(row_at, 1, split_three(-lse))
        extra = jnp.where(row_at == 0, 1.0, extra).astype(bf16)
        qaug_ref[...] = jnp.concatenate([high, low, extra], axis=0)
        grad_t = agrad_ref[part_rows]
        delta = jnp.sum(
            grad_t.astype(f32) * attended_ref[part_rows].astype(f32), axis=0, keepdims=True
        )
        grad_aug = jnp.concatenate(
            [grad_t, place(small_at, 0, split_three(-delta)).astype(bf16)], axis=0
        )
        def keys_step(at):
            pooled = pooled_ref[at]
            key_aug = key_blocks(pooled, wkt_ref[part_rows], aux_ref[at])
            key_t = dot(wkt_ref[part_rows], pooled, 1, 1).astype(bf16)
            value_h = dot(pooled, wvt_ref[part_rows], 1, 1).astype(bf16)
            value_aug = jnp.concatenate([value_h, three_ones], axis=1)
            probs = jnp.exp2(dot(key_aug, qaug_ref[...]))
            probs_grad = dot(value_aug, grad_aug)
            score_grad = (probs * probs_grad).astype(bf16)
            dv_ref[part_rows, at] = dot(grad_t, probs.astype(bf16), 1, 1).astype(bf16)
            dk_ref[part_rows, at] = (dot(head_queries, score_grad, 1, 1) * scale).astype(bf16)
            return dot(key_t, score_grad) * scale

        if keys == block:
            dq_ref[part_rows] = keys_step(pl.ds(0, keys)).astype(bf16)
        else:
            parts = keys // block
            total = lax.fori_loop(
                0,
                parts,
                lambda n, old: old + keys_step(pl.ds(pl.multiple_of(n * block, block), block)),
                jnp.zeros((size, tokens), f32),
            )
            dq_ref[part_rows] = total.astype(bf16)
        return carry

    lax.fori_loop(0, HEADS, head_step, 0)
    kwg_ref[...] = dot(dk_ref[...], pooled_ref[...]).astype(bf16)
    vwg_ref[...] = dot(dv_ref[...], pooled_ref[...]).astype(bf16)

    def pooled_step(n, carry):
        at = pl.ds(pl.multiple_of(n * 256, 256), 256)
        grad_t = dot(wk_ref[...], dk_ref[:, at]) + dot(wv_ref[...], dv_ref[:, at])
        pooled_out[at] = flipped(grad_t.astype(bf16))
        return carry

    lax.fori_loop(0, keys // 256, pooled_step, 0, unroll=min(4, keys // 256))
    qwg_ref[...] = dot(dq_ref[...], convq_ref[...]).astype(bf16)
    conv_grad_t = dot(wq_ref[...], dq_ref[...]).astype(bf16)
    for start in range(0, tokens, 256):
        cg_ref[start : start + 256] = flipped(conv_grad_t[:, start : start + 256])
    gain = gain_ref[...]
    bias = bias_ref[...]
    above, below = border_flags()
    ext = enc_ref.shape[0]
    units = []
    for e in range(ext):
        unit, inverse = norm_parts(enc_ref[e].astype(f32))
        z = (unit * gain + bias).astype(bf16).astype(f32)
        if e == 0:
            z = z * above
        if e == ext - 1:
            z = z * below
        units.append((unit, inverse, (z, from_left(z), from_right(z))))
    weights = poly_weights(conv_ref[...].astype(f32))
    tap_sum = [[0.0] * 3 for _ in range(3)]
    totals = [[None] * 3 for _ in range(ext)]
    row_sets = [{-1: [0], 0: [1, 2]}, {0: [0, 1], 1: [2]}]
    for i in range(ext - 2):
        for a in range(2):
            for b in range(2):
                at = ((2 * i + a) * 2 + b) * half
                cg = cg_ref[at : at + half].astype(f32)
                for (di, dj), w in weights[2 * a + b].items():
                    e = 1 + i + di
                    z = units[e][2][{0: 0, -1: 1, 1: 2}[dj]]
                    part = jnp.sum(cg * z, axis=0, keepdims=True)
                    for ti in row_sets[a][di]:
                        for tj in row_sets[b][dj]:
                            tap_sum[ti][tj] = tap_sum[ti][tj] + part
                    term = cg * w
                    old = totals[e][dj + 1]
                    totals[e][dj + 1] = term if old is None else old + term
    gain_sum = 0.0
    bias_sum = 0.0
    for e in range(ext):
        grad = totals[e][1] + from_right(totals[e][0]) + from_left(totals[e][2])
        if e == 0:
            grad = grad * above
        if e == ext - 1:
            grad = grad * below
        unit, inverse, _ = units[e]
        gain_sum = gain_sum + jnp.sum(grad * unit, axis=0, keepdims=True)
        bias_sum = bias_sum + jnp.sum(grad, axis=0, keepdims=True)
        result = norm_input_grad(grad, unit, inverse, gain)
        if 0 < e < ext - 1:
            for n in range(4):
                at = ((e - 1) * 4 + n) * half
                result = result + mgrad_ref[at : at + half]
        enc_out[e] = result.astype(bf16)
    vec_ref[...] = jnp.concatenate(
        [gain_sum, bias_sum]
        + [tap_sum[i][j] for i in range(3) for j in range(3)]
        + [gain2_sum, bias2_sum, jnp.zeros((3, width), f32)],
        axis=0,
    )


def attend_back(
    enc_ext, pooled_all, aux, gain, bias, conv_w, wq, wk, wv, wo, gain2, convq, queries, attended,
    lse, middle, cotp, sgrad, from_low, from_high,
):
    ext, half, width = enc_ext.shape
    tokens = convq.shape[0]
    keys = pooled_all.shape[0]
    size = width // HEADS
    square = jax.ShapeDtypeStruct((width, width), bf16)
    return pl.pallas_call(
        attend_back_kernel,
        out_shape=[
            jax.ShapeDtypeStruct((ext, half, width), bf16),
            jax.ShapeDtypeStruct((keys, width), bf16),
            square, square, square, square,
            jax.ShapeDtypeStruct((16, width), f32),
        ],
        scratch_shapes=[
            pltpu.VMEM((width, width), bf16),
            pltpu.VMEM((width, width), bf16),
            pltpu.VMEM((4 * size, tokens), bf16),
            pltpu.VMEM((tokens, width), f32),
            pltpu.VMEM((tokens, width), bf16),
            pltpu.VMEM((width, tokens), bf16),
            pltpu.VMEM((width, tokens), bf16),
            pltpu.VMEM((width, keys), bf16),
            pltpu.VMEM((width, keys), bf16),
            pltpu.VMEM((tokens, width), bf16),
        ],
        compiler_params=pltpu.CompilerParams(vmem_limit_bytes=VMEM),
        name="attend_backward",
    )(enc_ext, pooled_all, aux, gain, bias, conv_w, wq, wk, wv, wo, gain2, convq, queries, attended,
      lse, middle, cotp, sgrad, from_low, from_high)


def neighbours(low_part, high_part):
    count = lax.axis_size("band")
    forward = [(i, i + 1) for i in range(count - 1)]
    backward = [(target, source) for source, target in forward]
    return lax.ppermute(high_part, "band", forward), lax.ppermute(low_part, "band", backward)


def shards(
    encoded, key_mask, first_gain, first_bias, query_conv, query_weight, key_weight, value_weight,
    output_weight, second_gain, second_bias, up_weight, hidden_conv, down_weight, cotangent,
):
    bands = lax.axis_size("band")
    tasks = lax.axis_size("head")
    model = encoded.shape[3]
    _, rows, width, _ = cotangent.shape
    regrouped = lax.all_to_all(encoded, "band", split_axis=1, concat_axis=2, tiled=True)[0]
    from_low, from_high = neighbours(regrouped[:1], regrouped[-1:])
    enc_ext = jnp.concatenate([from_low, regrouped, from_high], axis=0)
    unit, _ = norm_parts(regrouped.astype(f32))
    normed = (unit * first_gain + first_bias).astype(bf16).astype(f32)
    coarse = regrouped.shape[1] * 2 // POOLC
    pooled = jnp.mean(
        normed.reshape(rows // POOLR, POOLR // 2, coarse, POOLC // 2, model), axis=(1, 3)
    ).astype(bf16).reshape(-1, model)
    pooled_all = lax.all_gather(pooled, ("band", "head"), axis=0, tiled=True)
    mask = jnp.where(key_mask > 0, 0.0, -1e9).reshape(bands, 1, rows // POOLR, coarse)
    mask = jnp.broadcast_to(mask, (bands, tasks, rows // POOLR, coarse)).reshape(-1, 1)
    lane = lax.broadcasted_iota(jnp.int32, (1, 128), 1)
    aux = jnp.where(lane == 0, mask, jnp.where(lane < 4, 1.0, 0.0)).astype(bf16)
    gain, bias = first_gain[None], first_bias[None]
    gain2, bias2 = second_gain[None], second_bias[None]
    convq, queries, attended, lse, middle, second = attend(
        enc_ext, pooled_all, aux, gain, bias, query_conv, query_weight, key_weight, value_weight,
        output_weight, gain2, bias2,
    )
    low, high = neighbours(second[:width], second[-width:])
    decoded, cotp, sgrad, upg, downg, hcg = feed_forward(
        second, low, high, middle, cotangent, up_weight, hidden_conv, down_weight
    )
    back_low, back_high = neighbours(
        sgrad[:width].astype(bf16), sgrad[-width:].astype(bf16)
    )
    enc_grad, pooled_grad, owg, qwg, kwg, vwg, vec = attend_back(
        enc_ext, pooled_all, aux, gain, bias, query_conv, query_weight, key_weight, value_weight,
        output_weight, gain2, convq, queries, attended, lse, middle, cotp, sgrad, back_low, back_high,
    )
    own = lax.psum_scatter(pooled_grad.astype(f32), ("band", "head"), scatter_dimension=0, tiled=True)
    unit, inverse = norm_parts(regrouped.astype(f32))
    spread = own.reshape(rows // POOLR, 1, coarse, 1, model) * (4.0 / (POOLR * POOLC))
    spread = jnp.broadcast_to(
        spread, (rows // POOLR, POOLR // 2, coarse, POOLC // 2, model)
    ).reshape(regrouped.shape)
    to_low, to_high = neighbours(enc_grad[:1], enc_grad[-1:])
    enc_own = (
        enc_grad[1:-1].astype(f32)
        + jnp.concatenate([to_low.astype(f32), to_high.astype(f32)], axis=0)
        + norm_input_grad(spread, unit, inverse, first_gain)
    )
    gain_grad = vec[0] + jnp.sum(spread * unit, axis=(0, 1))
    bias_grad = vec[1] + jnp.sum(spread, axis=(0, 1))
    encoded_grad = lax.all_to_all(
        enc_own.astype(bf16)[None], "band", split_axis=2, concat_axis=1, tiled=True
    )
    sums = lax.psum(
        tuple(
            x.astype(f32)
            for x in (gain_grad, bias_grad, vec[2:11], qwg, kwg, vwg, owg, vec[11], vec[12], upg, hcg, downg)
        ),
        ("band", "head"),
    )
    return (
        decoded, encoded_grad, sums[0], sums[1], sums[2], sums[3].T, sums[4].T, sums[5].T, sums[6],
        sums[7], sums[8], sums[9], sums[10], sums[11].T,
    )


def solution(mesh):
    split = P("head", None, "band", None)
    rows = P("head", "band", None, None)
    return jax.shard_map(
        shards, mesh=mesh, in_specs=(split,) + (P(),) * 13 + (rows,),
        out_specs=(rows, split) + (P(),) * 12, check_vma=False,
    )
```

```python
import functools
import math

import jax
import jax.numpy as jnp
from jax import lax
from jax.experimental import pallas as pl
from jax.experimental.pallas import tpu as pltpu
from jax.sharding import PartitionSpec as P

HEADS = 6
POOLR = 4
POOLC = 8
epsilon = 1e-06
f32 = jnp.float32
bf16 = jnp.bfloat16
VMEM = 60 << 20
MESH = pl.DeviceIdType.MESH


def dot(left, right, left_dim=1, right_dim=0):
    return lax.dot_general(
        left, right, (((left_dim,), (right_dim,)), ((), ())), preferred_element_type=f32
    )


def identity(size):
    rows = lax.broadcasted_iota(jnp.int32, (size, size), 0)
    cols = lax.broadcasted_iota(jnp.int32, (size, size), 1)
    return (rows == cols).astype(bf16)


def flipped(matrix):
    return matrix.T


def norm_parts(values):
    average = jnp.mean(values, axis=-1, keepdims=True)
    centered = values - average
    variance = jnp.mean(centered * centered, axis=-1, keepdims=True)
    inverse = lax.rsqrt(variance + epsilon)
    return centered * inverse, inverse


def norm_input_grad(upstream, unit_part, inverse, gain):
    scaled = upstream * gain
    average = jnp.mean(scaled, axis=-1, keepdims=True)
    projected = jnp.mean(scaled * unit_part, axis=-1, keepdims=True)
    return inverse * (scaled - average - unit_part * projected)


def from_left(block):
    rolled = pltpu.roll(block, 1, 0)
    rows = lax.broadcasted_iota(jnp.int32, block.shape, 0)
    return jnp.where(rows == 0, 0.0, rolled)


def from_right(block):
    count = block.shape[0]
    rolled = pltpu.roll(block, count - 1, 0)
    rows = lax.broadcasted_iota(jnp.int32, block.shape, 0)
    return jnp.where(rows == count - 1, 0.0, rolled)


def phase_order(width):
    half = width // 2
    rows = lax.broadcasted_iota(jnp.int32, (width, width), 0)
    cols = lax.broadcasted_iota(jnp.int32, (width, width), 1)
    wanted = jnp.where(rows < half, 2 * rows, 2 * (rows - half) + 1)
    return (cols == wanted).astype(bf16)


def split_three(values):
    high = values.astype(bf16)
    rest = values - high.astype(f32)
    middle = rest.astype(bf16)
    low = (rest - middle.astype(f32)).astype(bf16)
    return high, middle, low


def border_flags(dtype=f32):
    band = lax.axis_index("band")
    count = lax.axis_size("band")
    above = (band > 0).astype(dtype)
    below = (band < count - 1).astype(dtype)
    return above, below


def poly_weights(kernel):
    taps = [[kernel[3 * i + j : 3 * i + j + 1] for j in range(3)] for i in range(3)]
    row_sets = [{-1: [0], 0: [1, 2]}, {0: [0, 1], 1: [2]}]
    out = []
    for a in range(2):
        for b in range(2):
            entry = {}
            for di, rows in row_sets[a].items():
                for dj, cols in row_sets[b].items():
                    entry[(di, dj)] = functools.reduce(
                        lambda x, y: x + y, [taps[i][j] for i in rows for j in cols]
                    )
            out.append(entry)
    return out


def queries_kernel_part(enc_ref, gain, bias, conv_w, conv_ref):
    above, below = border_flags()
    rows = []
    for e in range(enc_ref.shape[0]):
        unit, _ = norm_parts(enc_ref[e].astype(f32))
        z = (unit * gain + bias).astype(bf16).astype(f32)
        if e == 0:
            z = z * above
        if e == enc_ref.shape[0] - 1:
            z = z * below
        rows.append((z, from_left(z), from_right(z)))
    weights = poly_weights(conv_w)
    half = rows[0][0].shape[0]
    at = 0
    for i in range(enc_ref.shape[0] - 2):
        for a in range(2):
            for b in range(2):
                total = None
                for (di, dj), w in weights[2 * a + b].items():
                    z = rows[1 + i + di][{0: 0, -1: 1, 1: 2}[dj]]
                    total = z * w if total is None else total + z * w
                conv_ref[at : at + half] = total.astype(bf16)
                at += half
    return rows


def key_blocks(pooled, key_t, aux):
    doubled = jnp.concatenate([key_t, key_t], axis=0)
    return jnp.concatenate([dot(pooled, doubled, 1, 1).astype(bf16), aux], axis=1)


def attend_kernel(
    enc_ref, pooled_ref, aux_ref, gain_ref, bias_ref, conv_ref, wq_ref, wk_ref, wv_ref, wo_ref,
    gain2_ref, bias2_ref,
    convq_ref, queries_ref, attended_ref, lse_ref, middle_ref, second_ref,
    wkt_ref, wvt_ref, qaug_ref, att_ref,
):
    keys = pooled_ref.shape[0]
    width = wq_ref.shape[0]
    tokens = convq_ref.shape[0]
    size = width // HEADS
    block = max(128, min(tokens, (1 << 20) // keys))
    queries_kernel_part(enc_ref, gain_ref[...], bias_ref[...], conv_ref[...].astype(f32), convq_ref)
    wkt_ref[...] = flipped(wk_ref[...])
    wvt_ref[...] = flipped(wv_ref[...])
    queries_t = dot(flipped(wq_ref[...]), convq_ref[...], 1, 1).astype(bf16)
    queries_ref[...] = queries_t
    factor = size ** (-0.5) * math.log2(math.e)
    ones_row = (lax.broadcasted_iota(jnp.int32, (size * 2, tokens), 0) == 0).astype(bf16)

    def head_step(h, carry):
        rows = pl.ds(pl.multiple_of(h * size, size), size)
        scaled = queries_ref[rows].astype(f32) * factor
        high = scaled.astype(bf16)
        low = (scaled - high.astype(f32)).astype(bf16)
        qaug_ref[...] = jnp.concatenate([high, low, ones_row], axis=0)
        key_aug = key_blocks(pooled_ref[...], wkt_ref[rows], aux_ref[...])
        value_t = dot(wvt_ref[rows], pooled_ref[...], 1, 1).astype(bf16)
        extra = (lax.broadcasted_iota(jnp.int32, (16, keys), 0) == 0).astype(bf16)
        value_aug = jnp.concatenate([value_t, extra], axis=0)
        for start in range(0, tokens, block):
            part = slice(start, start + block)
            scores = dot(key_aug, qaug_ref[:, part])
            top = jnp.max(scores, axis=0, keepdims=True)
            probs = jnp.exp2(scores - top).astype(bf16)
            mixed = dot(value_aug, probs)
            total = mixed[size : size + 1]
            normal = mixed[:size] / total
            attended_ref[rows, part] = normal
            att_ref[rows, part] = normal.astype(bf16)
            lse_ref[h, :, part] = jnp.broadcast_to(top + jnp.log2(total), (8, block))
        return carry

    lax.fori_loop(0, HEADS, head_step, 0)
    half = enc_ref.shape[1]
    for block_at in range(tokens // half):
        part = slice(block_at * half, (block_at + 1) * half)
        row = block_at // 4
        middle = enc_ref[1 + row].astype(f32) + dot(flipped(att_ref[:, part]), wo_ref[...])
        middle_ref[part] = middle
        unit, _ = norm_parts(middle)
        second_ref[part] = (unit * gain2_ref[...] + bias2_ref[...]).astype(bf16)


def attend(enc_ext, pooled_all, aux, gain, bias, conv_w, wq, wk, wv, wo, gain2, bias2):
    rows, half, width = enc_ext.shape
    tokens = (rows - 2) * 4 * half
    keys = pooled_all.shape[0]
    size = width // HEADS
    shapes = [
        jax.ShapeDtypeStruct((tokens, width), bf16),
        jax.ShapeDtypeStruct((width, tokens), bf16),
        jax.ShapeDtypeStruct((width, tokens), f32),
        jax.ShapeDtypeStruct((HEADS, 8, tokens), f32),
        jax.ShapeDtypeStruct((tokens, width), f32),
        jax.ShapeDtypeStruct((tokens, width), bf16),
    ]
    return pl.pallas_call(
        attend_kernel,
        out_shape=shapes,
        scratch_shapes=[
            pltpu.VMEM((width, width), bf16),
            pltpu.VMEM((width, width), bf16),
            pltpu.VMEM((4 * size, tokens), bf16),
            pltpu.VMEM((width, tokens), bf16),
        ],
        compiler_params=pltpu.CompilerParams(vmem_limit_bytes=VMEM),
        name="attend_forward",
    )(enc_ext, pooled_all, aux, gain, bias, conv_w, wq, wk, wv, wo, gain2, bias2)


def gelu_both(x):
    scale = math.sqrt(2.0 / math.pi)
    square = x * x
    inner = x * (scale + (scale * 0.044715) * square)
    t = jnp.tanh(inner)
    half = 0.5 * (1.0 + t)
    slope = half + (0.5 * x) * (1.0 - t * t) * (scale + (3.0 * scale * 0.044715) * square)
    return x * half, slope


def forward_kernel(
    own_ref, low_ref, high_ref, middle_ref, cot_ref, up_ref, hconv_ref, down_ref,
    decoded_ref, cotp_ref, sgrad_ref, upg_ref, downg_ref, hcg_ref,
    ext_ref, extt_ref, cott_ref, dec_ref, hid_ref, spr_ref,
):
    step = pl.program_id(0)
    steps = pl.num_programs(0)
    rows = cot_ref.shape[1]
    width = cot_ref.shape[2]
    half = width // 2
    tokens = rows * width

    @pl.when(step == 0)
    def _():
        ext_ref[0:width] = low_ref[...]
        ext_ref[width : width + tokens] = own_ref[...]
        ext_ref[width + tokens :] = high_ref[...]
        order = phase_order(width)
        for r in range(rows):
            cotp_ref[r * width : (r + 1) * width] = dot(order, cot_ref[0, r]).astype(bf16)
        for r in range(rows + 2):
            part = slice(r * width, (r + 1) * width)
            extt_ref[:, part] = flipped(ext_ref[part])
        for r in range(rows):
            part = slice(r * width, (r + 1) * width)
            cott_ref[:, part] = flipped(cotp_ref[part])
        dec_ref[...] = middle_ref[...]
        sgrad_ref[...] = jnp.zeros_like(sgrad_ref)

    up = up_ref[...]
    down = down_ref[...]
    weights = hconv_ref[...].astype(f32)
    taps = [[weights[3 * i + j : 3 * i + j + 1] for j in range(3)] for i in range(3)]
    hid_ref[...] = dot(ext_ref[...], up).astype(bf16)

    def phases(ref, r):
        even = ref[r * width : r * width + half].astype(f32)
        odd = ref[r * width + half : (r + 1) * width].astype(f32)
        return even, odd, from_left(odd), from_right(even)

    hid = [phases(hid_ref, r) for r in range(rows + 2)]
    act_grad = dot(cotp_ref[...], down, 1, 1)
    hcg = [[0.0] * 3 for _ in range(3)]
    acts = []
    grads = []
    for r in range(rows):
        for b in range(2):
            spread = None
            for i in range(3):
                even, odd, odd_left, even_right = hid[r + i]
                three = (odd_left, even, odd) if b == 0 else (even, odd, even_right)
                for j in range(3):
                    term = three[j] * taps[i][j]
                    spread = term if spread is None else spread + term
            act, slope = gelu_both(spread)
            at = r * width + b * half
            sg = (act_grad[at : at + half] * slope).astype(bf16)
            acts.append(act.astype(bf16))
            grads.append(sg)
            sgf = sg.astype(f32)
            for i in range(3):
                even, odd, odd_left, even_right = hid[r + i]
                three = (odd_left, even, odd) if b == 0 else (even, odd, even_right)
                for j in range(3):
                    hcg[i][j] = hcg[i][j] + jnp.sum(sgf * three[j], axis=0, keepdims=True)
    act_all = jnp.concatenate(acts, axis=0)
    dec_ref[...] += dot(act_all, down)
    downg_ref[...] = dot(cott_ref[...], act_all).astype(bf16)
    rest = jnp.zeros((hcg_ref.shape[0] - 9, up.shape[1]), f32)
    hcg_ref[...] = jnp.concatenate([hcg[i][j] for i in range(3) for j in range(3)] + [rest], axis=0)
    spr = []
    for r in range(rows):
        even = grads[2 * r].astype(f32)
        odd = grads[2 * r + 1].astype(f32)
        spr.append((even, odd, from_left(odd), from_right(even)))
    for r in range(-1, rows + 1):
        for b in range(2):
            total = None
            for i in range(3):
                source = r - i + 1
                if source < 0 or source >= rows:
                    continue
                even, odd, odd_left, even_right = spr[source]
                three = (odd, even, odd_left) if b == 0 else (even_right, odd, even)
                for j in range(3):
                    term = three[j] * taps[i][j]
                    total = term if total is None else total + term
            at = (r + 1) * width + b * half
            spr_ref[at : at + half] = total.astype(bf16)
    hid_grad = spr_ref[...]
    sgrad_ref[...] += dot(hid_grad, up, 1, 1)
    upg_ref[...] = dot(extt_ref[...], hid_grad).astype(bf16)

    @pl.when(step == steps - 1)
    def _():
        order = phase_order(width)
        for r in range(rows):
            part = slice(r * width, (r + 1) * width)
            decoded_ref[0, r] = dot(order, dec_ref[part].astype(bf16), 0, 0).astype(bf16)


def feed_forward(own, low, high, middle, cot, up, hconv, down):
    tokens, model = own.shape
    _, rows, width, _ = cot.shape
    hidden = up.shape[1]
    chunk = 256
    whole = lambda *shape: pl.BlockSpec(shape, lambda s: (0,) * len(shape))
    return pl.pallas_call(
        forward_kernel,
        grid=(hidden // chunk,),
        in_specs=[
            whole(tokens, model), whole(width, model), whole(width, model), whole(tokens, model),
            whole(1, rows, width, model),
            pl.BlockSpec((model, chunk), lambda s: (0, s)),
            pl.BlockSpec((9, chunk), lambda s: (0, s)),
            pl.BlockSpec((chunk, model), lambda s: (s, 0)),
        ],
        out_specs=[
            whole(1, rows, width, model), whole(tokens, model), whole(tokens + 2 * width, model),
            pl.BlockSpec((model, chunk), lambda s: (0, s)),
            pl.BlockSpec((model, chunk), lambda s: (0, s)),
            pl.BlockSpec((16, chunk), lambda s: (0, s)),
        ],
        out_shape=[
            jax.ShapeDtypeStruct((1, rows, width, model), bf16),
            jax.ShapeDtypeStruct((tokens, model), bf16),
            jax.ShapeDtypeStruct((tokens + 2 * width, model), f32),
            jax.ShapeDtypeStruct((model, hidden), bf16),
            jax.ShapeDtypeStruct((model, hidden), bf16),
            jax.ShapeDtypeStruct((16, hidden), f32),
        ],
        scratch_shapes=[
            pltpu.VMEM((tokens + 2 * width, model), bf16),
            pltpu.VMEM((model, tokens + 2 * width), bf16),
            pltpu.VMEM((model, tokens), bf16),
            pltpu.VMEM((tokens, model), f32),
            pltpu.VMEM((tokens + 2 * width, chunk), bf16),
            pltpu.VMEM((tokens + 2 * width, chunk), bf16),
        ],
        compiler_params=pltpu.CompilerParams(vmem_limit_bytes=VMEM),
        name="feed_forward",
    )(own, low, high, middle, cot, up, hconv, down)


def attend_back_kernel(
    enc_ref, pooled_ref, aux_ref, gain_ref, bias_ref, conv_ref, wq_ref, wk_ref, wv_ref, wo_ref,
    gain2_ref, convq_ref, queries_ref, attended_ref, lse_ref, middle_ref, cotp_ref, sgrad_ref,
    fromlow_ref, fromhigh_ref,
    enc_out, pooled_out, owg_ref, qwg_ref, kwg_ref, vwg_ref, vec_ref,
    wkt_ref, wvt_ref, qaug_ref, mgrad_ref, mlow_ref, agrad_ref, dq_ref, dk_ref, dv_ref, cg_ref,
):
    keys = pooled_ref.shape[0]
    tokens, width = convq_ref.shape
    size = width // HEADS
    half = enc_ref.shape[1]
    wide = 2 * half
    block = min(keys, 1024)
    gain2 = gain2_ref[...]
    gain2_sum = jnp.zeros((1, width), f32)
    bias2_sum = jnp.zeros((1, width), f32)
    rows = tokens // wide
    for r in range(rows):
        part = slice(r * wide, (r + 1) * wide)
        y = sgrad_ref[(r + 1) * wide : (r + 2) * wide]
        if r == 0:
            y = y + fromlow_ref[...].astype(f32)
        if r == rows - 1:
            y = y + fromhigh_ref[...].astype(f32)
        unit, inverse = norm_parts(middle_ref[part])
        gain2_sum += jnp.sum(y * unit, axis=0, keepdims=True)
        bias2_sum += jnp.sum(y, axis=0, keepdims=True)
        grad = cotp_ref[part].astype(f32) + norm_input_grad(y, unit, inverse, gain2)
        mgrad_ref[part] = grad
        mlow_ref[part] = grad.astype(bf16)
    owg_ref[...] = dot(attended_ref[...].astype(bf16), mlow_ref[...]).astype(bf16)
    agrad_ref[...] = dot(wo_ref[...], mlow_ref[...], 1, 1).astype(bf16)
    wkt_ref[...] = flipped(wk_ref[...])
    wvt_ref[...] = flipped(wv_ref[...])
    scale = size ** (-0.5)
    factor = scale * math.log2(math.e)
    row_at = lax.broadcasted_iota(jnp.int32, (2 * size, tokens), 0)
    small_at = lax.broadcasted_iota(jnp.int32, (size, tokens), 0)
    lane = lax.broadcasted_iota(jnp.int32, (block, size), 1)
    three_ones = (lane < 3).astype(bf16)

    def place(at, first, values):
        total = jnp.zeros(at.shape, f32)
        for n, value in enumerate(values):
            total = jnp.where(at == first + n, value.astype(f32), total)
        return total

    def head_step(h, carry):
        part_rows = pl.ds(pl.multiple_of(h * size, size), size)
        head_queries = queries_ref[part_rows]
        scaled = head_queries.astype(f32) * factor
        high = scaled.astype(bf16)
        low = (scaled - high.astype(f32)).astype(bf16)
        lse = lse_ref[h, 0:1, :]
        extra = place(row_at, 1, split_three(-lse))
        extra = jnp.where(row_at == 0, 1.0, extra).astype(bf16)
        qaug_ref[...] = jnp.concatenate([high, low, extra], axis=0)
        grad_t = agrad_ref[part_rows]
        delta = jnp.sum(
            grad_t.astype(f32) * attended_ref[part_rows], axis=0, keepdims=True
        )
        grad_aug = jnp.concatenate(
            [grad_t, place(small_at, 0, split_three(-delta)).astype(bf16)], axis=0
        )
        def keys_step(at):
            pooled = pooled_ref[at]
            key_aug = key_blocks(pooled, wkt_ref[part_rows], aux_ref[at])
            key_t = dot(wkt_ref[part_rows], pooled, 1, 1).astype(bf16)
            value_h = dot(pooled, wvt_ref[part_rows], 1, 1).astype(bf16)
            value_aug = jnp.concatenate([value_h, three_ones], axis=1)
            probs = jnp.exp2(dot(key_aug, qaug_ref[...]))
            probs_grad = dot(value_aug, grad_aug)
            score_grad = (probs * probs_grad).astype(bf16)
            dv_ref[part_rows, at] = dot(grad_t, probs.astype(bf16), 1, 1).astype(bf16)
            dk_ref[part_rows, at] = (dot(head_queries, score_grad, 1, 1) * scale).astype(bf16)
            return dot(key_t, score_grad) * scale

        if keys == block:
            dq_ref[part_rows] = keys_step(pl.ds(0, keys)).astype(bf16)
        else:
            parts = keys // block
            total = lax.fori_loop(
                0,
                parts,
                lambda n, old: old + keys_step(pl.ds(pl.multiple_of(n * block, block), block)),
                jnp.zeros((size, tokens), f32),
            )
            dq_ref[part_rows] = total.astype(bf16)
        return carry

    lax.fori_loop(0, HEADS, head_step, 0)
    kwg_ref[...] = dot(dk_ref[...], pooled_ref[...]).astype(bf16)
    vwg_ref[...] = dot(dv_ref[...], pooled_ref[...]).astype(bf16)

    def pooled_step(n, carry):
        at = pl.ds(pl.multiple_of(n * 256, 256), 256)
        grad_t = dot(wk_ref[...], dk_ref[:, at]) + dot(wv_ref[...], dv_ref[:, at])
        pooled_out[at] = flipped(grad_t.astype(bf16))
        return carry

    lax.fori_loop(0, keys // 256, pooled_step, 0, unroll=min(4, keys // 256))
    qwg_ref[...] = dot(dq_ref[...], convq_ref[...]).astype(bf16)
    conv_grad_t = dot(wq_ref[...], dq_ref[...]).astype(bf16)
    for start in range(0, tokens, 256):
        cg_ref[start : start + 256] = flipped(conv_grad_t[:, start : start + 256])
    gain = gain_ref[...]
    bias = bias_ref[...]
    above, below = border_flags()
    ext = enc_ref.shape[0]
    units = []
    for e in range(ext):
        unit, inverse = norm_parts(enc_ref[e].astype(f32))
        z = (unit * gain + bias).astype(bf16).astype(f32)
        if e == 0:
            z = z * above
        if e == ext - 1:
            z = z * below
        units.append((unit, inverse, (z, from_left(z), from_right(z))))
    weights = poly_weights(conv_ref[...].astype(f32))
    tap_sum = [[0.0] * 3 for _ in range(3)]
    totals = [[None] * 3 for _ in range(ext)]
    row_sets = [{-1: [0], 0: [1, 2]}, {0: [0, 1], 1: [2]}]
    for i in range(ext - 2):
        for a in range(2):
            for b in range(2):
                at = ((2 * i + a) * 2 + b) * half
                cg = cg_ref[at : at + half].astype(f32)
                for (di, dj), w in weights[2 * a + b].items():
                    e = 1 + i + di
                    z = units[e][2][{0: 0, -1: 1, 1: 2}[dj]]
                    part = jnp.sum(cg * z, axis=0, keepdims=True)
                    for ti in row_sets[a][di]:
                        for tj in row_sets[b][dj]:
                            tap_sum[ti][tj] = tap_sum[ti][tj] + part
                    term = cg * w
                    old = totals[e][dj + 1]
                    totals[e][dj + 1] = term if old is None else old + term
    gain_sum = 0.0
    bias_sum = 0.0
    for e in range(ext):
        grad = totals[e][1] + from_right(totals[e][0]) + from_left(totals[e][2])
        if e == 0:
            grad = grad * above
        if e == ext - 1:
            grad = grad * below
        unit, inverse, _ = units[e]
        gain_sum = gain_sum + jnp.sum(grad * unit, axis=0, keepdims=True)
        bias_sum = bias_sum + jnp.sum(grad, axis=0, keepdims=True)
        result = norm_input_grad(grad, unit, inverse, gain)
        if 0 < e < ext - 1:
            for n in range(4):
                at = ((e - 1) * 4 + n) * half
                result = result + mgrad_ref[at : at + half]
        enc_out[e] = result.astype(bf16)
    vec_ref[...] = jnp.concatenate(
        [gain_sum, bias_sum]
        + [tap_sum[i][j] for i in range(3) for j in range(3)]
        + [gain2_sum, bias2_sum, jnp.zeros((3, width), f32)],
        axis=0,
    )


def attend_back(
    enc_ext, pooled_all, aux, gain, bias, conv_w, wq, wk, wv, wo, gain2, convq, queries, attended,
    lse, middle, cotp, sgrad, from_low, from_high,
):
    ext, half, width = enc_ext.shape
    tokens = convq.shape[0]
    keys = pooled_all.shape[0]
    size = width // HEADS
    square = jax.ShapeDtypeStruct((width, width), bf16)
    return pl.pallas_call(
        attend_back_kernel,
        out_shape=[
            jax.ShapeDtypeStruct((ext, half, width), bf16),
            jax.ShapeDtypeStruct((keys, width), bf16),
            square, square, square, square,
            jax.ShapeDtypeStruct((16, width), f32),
        ],
        scratch_shapes=[
            pltpu.VMEM((width, width), bf16),
            pltpu.VMEM((width, width), bf16),
            pltpu.VMEM((4 * size, tokens), bf16),
            pltpu.VMEM((tokens, width), f32),
            pltpu.VMEM((tokens, width), bf16),
            pltpu.VMEM((width, tokens), bf16),
            pltpu.VMEM((width, tokens), bf16),
            pltpu.VMEM((width, keys), bf16),
            pltpu.VMEM((width, keys), bf16),
            pltpu.VMEM((tokens, width), bf16),
        ],
        compiler_params=pltpu.CompilerParams(vmem_limit_bytes=VMEM),
        name="attend_backward",
    )(enc_ext, pooled_all, aux, gain, bias, conv_w, wq, wk, wv, wo, gain2, convq, queries, attended,
      lse, middle, cotp, sgrad, from_low, from_high)


def bit_of(axis, bit):
    return lax.rem(lax.div(lax.axis_index(axis), 1 << bit), 2)


def partner(axis, bit):
    at = lax.axis_index(axis)
    return {axis: at + (1 - 2 * bit_of(axis, bit)) * (1 << bit)}


def greet(targets):
    barrier = pltpu.get_barrier_semaphore()
    for target in targets:
        pl.semaphore_signal(barrier, inc=1, device_id=target, device_id_type=MESH)
    pl.semaphore_wait(barrier, len(targets))


def band_peers(bands):
    at = lax.axis_index("band")
    return [lax.rem(at + n, bands) for n in range(1, bands)]


LINKS = (("band", 2), ("band", 1), ("band", 0), ("head", 1), ("head", 0))


def link_targets():
    return [partner(axis, bit) for axis, bit in LINKS]


def greet_all(bands):
    targets = [{"band": peer} for peer in band_peers(bands)]
    greet(targets + [partner("head", 1), partner("head", 0)])


class Doubling:
    def __init__(self, ref, columns, links, send, recv, first):
        self.ref, self.columns, self.links = ref, columns, links
        self.send, self.recv, self.first = send, recv, first
        self.block = ref.shape[0] >> len(links)
        self.copies = {}

    def own_start(self):
        start = 0
        for n, link in enumerate(self.links):
            start = start + bit_of(*link) * (self.block << n)
        return pl.multiple_of(start, 16)

    def view(self, start, count):
        rows = pl.ds(pl.multiple_of(start, 16), count)
        return self.ref.at[rows, self.columns] if self.columns else self.ref.at[rows]

    def start(self, n):
        start = 0
        for m, link in enumerate(self.links):
            if m >= n:
                start = start + bit_of(*link) * (self.block << m)
        view = self.view(start, self.block << n)
        self.copies[n] = pltpu.make_async_remote_copy(
            src_ref=view, dst_ref=view, send_sem=self.send.at[self.first + n],
            recv_sem=self.recv.at[self.first + n], device_id=partner(*self.links[n]),
            device_id_type=MESH,
        )
        self.copies[n].start()

    def finish(self, n):
        self.copies[n].wait()


class Halving:
    def __init__(self, ref, columns, links, landing, send, recv, first):
        self.ref, self.columns, self.links = ref, columns, links
        self.landing, self.send, self.recv, self.first = landing, send, recv, first
        self.rows = ref.shape[0]
        self.copies = {}
        self.keep = {}

    def view(self, start, count):
        rows = pl.ds(pl.multiple_of(start, 16), count)
        return (rows, self.columns) if self.columns else (rows, slice(None))

    def begin(self, n):
        start = 0
        for m in range(n):
            start = start + bit_of(*self.links[m]) * (self.rows >> (m + 1))
        return start

    def start(self, n):
        half = self.rows >> (n + 1)
        start = self.begin(n)
        bit = bit_of(*self.links[n])
        out = self.view(start + (1 - bit) * half, half)
        land = self.landing.at[pl.ds(self.rows - 2 * half, half), self.view(0, half)[1]]
        self.copies[n] = pltpu.make_async_remote_copy(
            src_ref=self.ref.at[out], dst_ref=land, send_sem=self.send.at[self.first + n],
            recv_sem=self.recv.at[self.first + n], device_id=partner(*self.links[n]),
            device_id_type=MESH,
        )
        self.copies[n].start()

    def finish(self, n, last=None):
        half = self.rows >> (n + 1)
        keep = self.view(self.begin(n + 1), half)
        self.copies[n].wait()
        land = self.landing[pl.ds(self.rows - 2 * half, half), self.view(0, half)[1]]
        total = self.ref[keep].astype(f32) + land.astype(f32)
        if last is None:
            self.ref[keep] = total.astype(self.ref.dtype)
        else:
            last(total)


def start_kernel(enc_ref, gain_ref, bias_ref, ext_ref, pooled_ref, padded_ref, send, recv, gsend, grecv):
    bands = lax.axis_size("band")
    me = lax.axis_index("band")
    _, height, columns, model = enc_ref.shape
    rows = ext_ref.shape[0]
    own_rows = rows - 2
    padded_ref[0] = jnp.zeros((columns, model), bf16)
    padded_ref[height + 1] = jnp.zeros((columns, model), bf16)
    padded_ref[1 : height + 1] = enc_ref[0]
    greet_all(bands)
    mine = pl.ds(pl.multiple_of(me * columns, 16), columns)
    copies = []
    for n, peer in enumerate(band_peers(bands)):
        copy = pltpu.make_async_remote_copy(
            src_ref=padded_ref.at[pl.ds(peer * own_rows, rows)], dst_ref=ext_ref.at[:, mine],
            send_sem=send.at[n], recv_sem=recv.at[n], device_id={"band": peer}, device_id_type=MESH,
        )
        copy.start()
        copies.append(copy)
    ext_ref[:, mine] = padded_ref[pl.ds(me * own_rows, rows)]
    for copy in copies:
        copy.wait()
    half = ext_ref.shape[1]
    cells = half // (POOLC // 2)
    pick = lax.broadcasted_iota(jnp.int32, (cells, half), 0)
    column = lax.broadcasted_iota(jnp.int32, (cells, half), 1)
    first = pick * (POOLC // 2)
    mean = jnp.where(
        (column >= first) & (column < first + POOLC // 2), 4.0 / (POOLR * POOLC), 0.0
    ).astype(bf16)
    total = 0.0
    for e in range(1, rows - 1):
        unit, _ = norm_parts(ext_ref[e].astype(f32))
        z = (unit * gain_ref[...] + bias_ref[...]).astype(bf16)
        total = total + dot(mean, z)
    gather = Doubling(pooled_ref, None, LINKS, gsend, grecv, 0)
    pooled_ref[pl.ds(gather.own_start(), cells)] = total.astype(bf16)
    for n in range(len(LINKS)):
        gather.start(n)
        gather.finish(n)


def start_transfers(encoded, gain, bias, bands, devices):
    _, height, columns, model = encoded.shape
    own_rows = height // bands
    half = columns * bands
    cells = half // (POOLC // 2)
    return pl.pallas_call(
        start_kernel,
        out_shape=[
            jax.ShapeDtypeStruct((own_rows + 2, half, model), bf16),
            jax.ShapeDtypeStruct((cells * devices, model), bf16),
        ],
        scratch_shapes=[
            pltpu.VMEM((height + 2, columns, model), bf16),
            pltpu.SemaphoreType.DMA((bands - 1,)),
            pltpu.SemaphoreType.DMA((bands - 1,)),
            pltpu.SemaphoreType.DMA((len(LINKS),)),
            pltpu.SemaphoreType.DMA((len(LINKS),)),
        ],
        compiler_params=pltpu.CompilerParams(
            vmem_limit_bytes=VMEM, collective_id=1, has_side_effects=True
        ),
        name="start_transfers",
    )(encoded, gain, bias)


Z_HIGH, Z_LOW, Y, X, CORE = LINKS
ORDERS = (
    (CORE, X, Y, Z_LOW, Z_HIGH),
    (CORE, Y, Z_LOW, Z_HIGH, X),
    (CORE, Z_LOW, Z_HIGH, X, Y),
)
WIDE = 2304
NARROW = 1280


def end_kernel(
    up_ref, down_ref, query_ref, key_ref, value_ref, output_ref, vec_ref, hconv_ref, pooled_ref,
    encg_ref, ext_ref, gain_ref,
    wide_out, narrow_out, enc_out, tiny_out,
    wide_ref, narrow_ref, wide_land, narrow_land, pooled_sum, pooled_land, enc_send, enc_land,
    tiny, tiny_land, local, send, recv, asend, arecv, tsend, trecv,
):
    bands = lax.axis_size("band")
    me = lax.axis_index("band")
    model = gain_ref.shape[1]
    loads = []

    def load(source, target):
        copy = pltpu.make_async_copy(source, target, local.at[len(loads)])
        copy.start()
        loads.append(copy)

    load(up_ref, wide_ref.at[pl.ds(0, 384), pl.ds(0, 1536)])
    load(down_ref.at[:, pl.ds(0, 768)], wide_ref.at[pl.ds(0, 384), pl.ds(1536, 768)])
    for n in range(3):
        load(
            down_ref.at[pl.ds(128 * n, 128), pl.ds(768, 768)],
            wide_ref.at[pl.ds(384, 128), pl.ds(768 * n, 768)],
        )
    for n, square in enumerate((query_ref, key_ref, value_ref)):
        load(square, narrow_ref.at[pl.ds(0, 384), pl.ds(384 * n, 384)])
        load(
            output_ref.at[pl.ds(128 * n, 128)],
            narrow_ref.at[pl.ds(384, 128), pl.ds(384 * n, 384)],
        )
    load(pooled_ref, pooled_sum)
    greet_all(bands)
    for n in range(15):
        small = vec_ref if n < 3 else hconv_ref
        at = 128 * (n if n < 3 else n - 3)
        narrow_ref[16 * n : 16 * n + 16, 1152:1280] = small[:, at : at + 128].astype(bf16)
    narrow_ref[240:512, 1152:1280] = jnp.zeros((272, 128), bf16)
    for copy in loads:
        copy.wait()
    parts = []
    count = len(LINKS)

    def add(ref, columns, links, landing):
        parts.append(Halving(ref, columns, links, landing, send, recv, count * len(parts)))

    pooled = Halving(pooled_sum, None, LINKS[::-1], pooled_land, send, recv, 0)
    parts.append(pooled)
    for n in range(3):
        add(narrow_ref, pl.ds((0, 384, 768)[n], (384, 384, 512)[n]), ORDERS[n], narrow_land)
    for n in range(3):
        add(wide_ref, pl.ds(768 * n, 768), ORDERS[n], wide_land)
    outs = []
    for n in range(3):
        first = 5 * (7 + len(outs))
        outs.append(Doubling(narrow_out, pl.ds((0, 384, 768)[n], (384, 384, 512)[n]), ORDERS[n][::-1], send, recv, first))
    for n in range(3):
        first = 5 * (7 + len(outs))
        outs.append(Doubling(wide_out, pl.ds(768 * n, 768), ORDERS[n][::-1], send, recv, first))
    for part in parts:
        part.start(0)
    rows = ext_ref.shape[0]
    own_rows = rows - 2
    half = ext_ref.shape[1]
    units = [norm_parts(ext_ref[1 + e].astype(f32)) for e in range(own_rows)]
    cells = half // (POOLC // 2)
    cell = lax.broadcasted_iota(jnp.int32, (half, cells), 0)
    first = lax.broadcasted_iota(jnp.int32, (half, cells), 1) * (POOLC // 2)
    widen = jnp.where((cell >= first) & (cell < first + POOLC // 2), 1.0, 0.0).astype(bf16)
    for n in range(count):
        for at, part in enumerate(parts):
            if n < count - 1:
                part.finish(n)
                part.start(n + 1)

    def pooled_last(total):
        spread = 0.0
        for piece in split_three(total * (4.0 / (POOLR * POOLC))):
            spread = spread + dot(widen, piece)
        gain = gain_ref[...]
        gain_sum = 0.0
        for e in range(own_rows):
            unit, inverse = units[e]
            grad = encg_ref[1 + e].astype(f32) + norm_input_grad(spread, unit, inverse, gain)
            for band in range(bands):
                enc_send[band, 1 + e] = grad[band * 16 : band * 16 + 16].astype(bf16)
            gain_sum = gain_sum + jnp.sum(spread * unit, axis=0, keepdims=True)
        for e in (0, rows - 1):
            for band in range(bands):
                enc_send[band, e] = encg_ref[e, band * 16 : band * 16 + 16]
        bias_sum = own_rows * jnp.sum(spread, axis=0, keepdims=True)
        tiny[0] = jnp.concatenate([gain_sum, bias_sum, jnp.zeros((6, model), f32)], axis=0)

    pooled.finish(count - 1, pooled_last)
    copies = []
    for n, peer in enumerate(band_peers(bands)):
        copy = pltpu.make_async_remote_copy(
            src_ref=enc_send.at[peer], dst_ref=enc_land.at[me], send_sem=asend.at[n],
            recv_sem=arecv.at[n], device_id={"band": peer}, device_id_type=MESH,
        )
        copy.start()
        copies.append(copy)
    enc_land[me] = enc_send[me]
    for part, out in zip(parts[1:], outs):

        def write(total, out=out):
            out.ref[pl.ds(out.own_start(), 16), out.columns] = total.astype(bf16)

        part.finish(count - 1, write)
        out.start(0)
    for n in range(count):
        copy = pltpu.make_async_remote_copy(
            src_ref=tiny.at[n], dst_ref=tiny_land.at[n], send_sem=tsend.at[n],
            recv_sem=trecv.at[n], device_id=partner(*LINKS[n]), device_id_type=MESH,
        )
        copy.start()
        for out in outs:
            out.finish(n)
            if n < count - 1:
                out.start(n + 1)
        copy.wait()
        tiny[n + 1] = tiny[n] + tiny_land[n]
        if n == 0:
            for block in copies:
                block.wait()
            for band in range(bands):
                for e in range(own_rows):
                    grad = enc_land[band, 1 + e].astype(f32)
                    if e == 0 and band > 0:
                        grad = grad + enc_land[band - 1, rows - 1].astype(f32)
                    if e == own_rows - 1 and band < bands - 1:
                        grad = grad + enc_land[band + 1, 0].astype(f32)
                    enc_out[0, own_rows * band + e] = grad.astype(bf16)
    tiny_out[...] = tiny[count]


def end_transfers(up, down, query, key, value, output, vec, hconv, pooled, enc_grad, ext, gain, bands):
    ext_rows, half, model = ext.shape
    any_space = pl.BlockSpec(memory_space=pl.ANY)
    vmem = pl.BlockSpec(memory_space=pltpu.VMEM)
    columns = half // bands
    height = (ext_rows - 2) * bands
    return pl.pallas_call(
        end_kernel,
        in_specs=[any_space] * 6 + [vmem, vmem, any_space, vmem, vmem, vmem],
        out_shape=[
            jax.ShapeDtypeStruct((512, WIDE), bf16),
            jax.ShapeDtypeStruct((512, NARROW), bf16),
            jax.ShapeDtypeStruct((1, height, columns, model), bf16),
            jax.ShapeDtypeStruct((8, model), f32),
        ],
        scratch_shapes=[
            pltpu.VMEM((512, WIDE), bf16),
            pltpu.VMEM((512, NARROW), bf16),
            pltpu.VMEM((512, WIDE), bf16),
            pltpu.VMEM((512, NARROW), bf16),
            pltpu.VMEM(pooled.shape, bf16),
            pltpu.VMEM(pooled.shape, bf16),
            pltpu.VMEM((bands, ext_rows, columns, model), bf16),
            pltpu.VMEM((bands, ext_rows, columns, model), bf16),
            pltpu.VMEM((len(LINKS) + 1, 8, model), f32),
            pltpu.VMEM((len(LINKS), 8, model), f32),
            pltpu.SemaphoreType.DMA((12,)),
            pltpu.SemaphoreType.DMA((65,)),
            pltpu.SemaphoreType.DMA((65,)),
            pltpu.SemaphoreType.DMA((bands - 1,)),
            pltpu.SemaphoreType.DMA((bands - 1,)),
            pltpu.SemaphoreType.DMA((len(LINKS),)),
            pltpu.SemaphoreType.DMA((len(LINKS),)),
        ],
        compiler_params=pltpu.CompilerParams(
            vmem_limit_bytes=VMEM, collective_id=2, has_side_effects=True
        ),
        name="end_transfers",
    )(up, down, query, key, value, output, vec, hconv, pooled, enc_grad, ext, gain)


def widen_kernel(
    wide_ref, narrow_ref, tiny_ref, enc_ref,
    enc_out, gain_out, bias_out, conv_out, query_out, key_out, value_out, output_out, gain2_out,
    bias2_out, up_out, hconv_out, down_out,
):
    enc_out[...] = enc_ref[...]
    small = jnp.concatenate(
        [narrow_ref[16 * n : 16 * n + 16, 1152:1280].astype(f32) for n in range(3)], axis=1
    )
    gain_out[...] = (small[0:1] + tiny_ref[0:1])[0]
    bias_out[...] = (small[1:2] + tiny_ref[1:2])[0]
    conv_out[...] = small[2:11]
    gain2_out[...] = small[11:12][0]
    bias2_out[...] = small[12:13][0]
    for n in range(12):
        rows = narrow_ref[48 + 16 * n : 64 + 16 * n, 1152:1280].astype(f32)
        hconv_out[:, 128 * n : 128 * n + 128] = rows[0:9]
    for n, out in enumerate((query_out, key_out, value_out)):
        out[...] = flipped(narrow_ref[0:384, 384 * n : 384 * n + 384]).astype(f32)
        output_out[128 * n : 128 * n + 128] = narrow_ref[384:512, 384 * n : 384 * n + 384].astype(f32)
        down_out[768:1536, 128 * n : 128 * n + 128] = flipped(
            wide_ref[384:512, 768 * n : 768 * n + 768]
        ).astype(f32)
    up_out[...] = wide_ref[0:384, 0:1536].astype(f32)
    down_out[0:768] = flipped(wide_ref[0:384, 1536:2304]).astype(f32)


def widened(wide, narrow, tiny, enc):
    model = tiny.shape[1]
    hidden = 4 * model
    vector = jax.ShapeDtypeStruct((model,), f32)
    square = jax.ShapeDtypeStruct((model, model), f32)
    return pl.pallas_call(
        widen_kernel,
        out_shape=[
            jax.ShapeDtypeStruct(enc.shape, bf16), vector, vector,
            jax.ShapeDtypeStruct((9, model), f32), square, square, square, square, vector, vector,
            jax.ShapeDtypeStruct((model, hidden), f32), jax.ShapeDtypeStruct((9, hidden), f32),
            jax.ShapeDtypeStruct((hidden, model), f32),
        ],
        compiler_params=pltpu.CompilerParams(vmem_limit_bytes=VMEM),
        name="widen",
    )(wide, narrow, tiny, enc)


def neighbours(low_part, high_part):
    count = lax.axis_size("band")
    forward = [(i, i + 1) for i in range(count - 1)]
    backward = [(target, source) for source, target in forward]
    return lax.ppermute(high_part, "band", forward), lax.ppermute(low_part, "band", backward)


def start_plain(encoded, gain, bias, rows, coarse):
    model = encoded.shape[3]
    regrouped = lax.all_to_all(encoded, "band", split_axis=1, concat_axis=2, tiled=True)[0]
    from_low, from_high = neighbours(regrouped[:1], regrouped[-1:])
    enc_ext = jnp.concatenate([from_low, regrouped, from_high], axis=0)
    unit, _ = norm_parts(regrouped.astype(f32))
    normed = (unit * gain + bias).astype(bf16).astype(f32)
    pooled = jnp.mean(
        normed.reshape(rows // POOLR, POOLR // 2, coarse, POOLC // 2, model), axis=(1, 3)
    ).astype(bf16).reshape(-1, model)
    return enc_ext, regrouped, lax.all_gather(pooled, ("band", "head"), axis=0, tiled=True)


def shards(
    encoded, key_mask, first_gain, first_bias, query_conv, query_weight, key_weight, value_weight,
    output_weight, second_gain, second_bias, up_weight, hidden_conv, down_weight, cotangent,
):
    bands = lax.axis_size("band")
    tasks = lax.axis_size("head")
    model = encoded.shape[3]
    _, rows, width, _ = cotangent.shape
    own_kernels = (bands, tasks, model, up_weight.shape[1]) == (8, 4, 384, 1536)
    gain, bias = first_gain[None], first_bias[None]
    gain2, bias2 = second_gain[None], second_bias[None]
    coarse = width // POOLC
    mask = jnp.where(key_mask > 0, 0.0, -1e9).reshape(bands, 1, rows // POOLR, coarse)
    if own_kernels:
        mask = mask.reshape(2, 2, 2, rows // POOLR * coarse).transpose(2, 1, 0, 3)
        mask = jnp.broadcast_to(
            mask.reshape(1, bands, rows // POOLR, coarse), (tasks, bands, rows // POOLR, coarse)
        )
        enc_ext, pooled_all = start_transfers(encoded, gain, bias, bands, bands * tasks)
    else:
        mask = jnp.broadcast_to(mask, (bands, tasks, rows // POOLR, coarse))
        enc_ext, regrouped, pooled_all = start_plain(encoded, first_gain, first_bias, rows, coarse)
    lane = lax.broadcasted_iota(jnp.int32, (1, 128), 1)
    aux = jnp.where(
        lane == 0, mask.reshape(-1, 1), jnp.where(lane < 4, 1.0, 0.0)
    ).astype(bf16)
    convq, queries, attended, lse, middle, second = attend(
        enc_ext, pooled_all, aux, gain, bias, query_conv, query_weight, key_weight, value_weight,
        output_weight, gain2, bias2,
    )
    low, high = neighbours(second[:width], second[-width:])
    decoded, cotp, sgrad, upg, downg, hcg = feed_forward(
        second, low, high, middle, cotangent, up_weight, hidden_conv, down_weight
    )
    back_low, back_high = neighbours(
        sgrad[:width].astype(bf16), sgrad[-width:].astype(bf16)
    )
    enc_grad, pooled_grad, owg, qwg, kwg, vwg, vec = attend_back(
        enc_ext, pooled_all, aux, gain, bias, query_conv, query_weight, key_weight, value_weight,
        output_weight, gain2, convq, queries, attended, lse, middle, cotp, sgrad, back_low, back_high,
    )
    if own_kernels:
        wide, narrow, enc_sum, tiny = end_transfers(
            upg, downg, qwg, kwg, vwg, owg, vec, hcg, pooled_grad, enc_grad, enc_ext, gain, bands
        )
        return (decoded, *widened(wide, narrow, tiny, enc_sum))
    own = lax.psum_scatter(pooled_grad.astype(f32), ("band", "head"), scatter_dimension=0, tiled=True)
    unit, inverse = norm_parts(regrouped.astype(f32))
    spread = own.reshape(rows // POOLR, 1, coarse, 1, model) * (4.0 / (POOLR * POOLC))
    spread = jnp.broadcast_to(
        spread, (rows // POOLR, POOLR // 2, coarse, POOLC // 2, model)
    ).reshape(regrouped.shape)
    to_low, to_high = neighbours(enc_grad[:1], enc_grad[-1:])
    enc_own = (
        enc_grad[1:-1].astype(f32)
        + jnp.concatenate([to_low.astype(f32), to_high.astype(f32)], axis=0)
        + norm_input_grad(spread, unit, inverse, first_gain)
    )
    gain_grad = vec[0] + jnp.sum(spread * unit, axis=(0, 1))
    bias_grad = vec[1] + jnp.sum(spread, axis=(0, 1))
    encoded_grad = lax.all_to_all(
        enc_own.astype(bf16)[None], "band", split_axis=2, concat_axis=1, tiled=True
    )
    sums = lax.psum(
        tuple(
            x.astype(f32)
            for x in (gain_grad, bias_grad, vec[2:11], qwg, kwg, vwg, owg, vec[11], vec[12], upg, hcg[:9], downg)
        ),
        ("band", "head"),
    )
    return (
        decoded, encoded_grad, sums[0], sums[1], sums[2], sums[3].T, sums[4].T, sums[5].T, sums[6],
        sums[7], sums[8], sums[9], sums[10], sums[11].T,
    )


def solution(mesh):
    split = P("head", None, "band", None)
    rows = P("head", "band", None, None)
    return jax.shard_map(
        shards, mesh=mesh, in_specs=(split,) + (P(),) * 13 + (rows,),
        out_specs=(rows, split) + (P(),) * 12, check_vma=False,
    )
```
